256 devices in a mesh: group: 8 (over x, z_lo), shard: 32 (over y, z_hi, core).
Axes of the slice: x: 4, y: 4, z: 8 (z_hi: 4, z_lo: 2; z = z_hi * 2 + z_lo), core: 2. Of those that a mesh axis runs over, the one named last changes fastest.
Arguments:
- numerators: float32 [8, 128, 5120], P('group', 'shard'), may hold values from -6 to 6
- push_weight: float32 [8], P('group'), may hold values from 0.5 to 2
- keep_share: float32 [8], P('group'), may hold values from 0.25 to 0.75
- momentum: float32 [8, 128, 5120], P('group', 'shard'), may hold values from -4 to 4
- grads: float32 [3, 8, 32, 128, 5120], P(None, 'group', 'shard'), may hold values from -6 to 6
Outputs:
- displacement: float32 [8, 128, 5120], P('group', 'shard')
- momentum_out: float32 [8, 128, 5120], P('group', 'shard')
- weight_out: float32 [8], P('group')
The draws below stay inside these ranges and needn't reach their ends.
All inputs are finite; a program needn't handle non-finite values.
Results may differ from the reference program's by a relative error of at most 0.0001.
Values sent between devices are 32-bit elements; how exact they have to be, the bound alone decides.
No kernel may reach another device: no remote copies, remote signals or barrier semaphores. Data moves between devices by JAX's collectives and lax.ppermute only.
A program may use at most 64 MiB of HBM per device.

```python
import math
import jax
import jax.numpy as jnp

D = 5120
STEPS = 3
ROWS = 128
N_GROUP = 8
N_SHARD = 32


def strengthened(array, rng, source, target, shards_of, factor):
    def block_of(axis_at):
        return (jnp.arange(array.shape[axis_at]) // (array.shape[axis_at] // shards_of)).reshape((-1,) + (1,) * (array.ndim - 1 - axis_at))

    one_side = jax.random.permutation(rng, shards_of)[block_of(target)]
    other_side = (block_of(target) + shards_of // 2) % shards_of
    return jnp.where((block_of(source) == one_side) | (block_of(source) == other_side), factor * array, array)


def shard_levels(rng, extent, pieces, low, top_value):
    def one(dim, parts):
        heights = jax.random.uniform(jax.random.fold_in(jax.random.fold_in(rng, 6), dim), (parts,), jnp.float32, low / len(pieces), top_value / len(pieces))
        return jnp.repeat(jnp.exp(heights), extent[dim] // parts).reshape((-1,) + (1,) * (len(extent) - dim - 1))

    factor_of = one(*pieces[0])
    for cut in pieces[1:]:
        factor_of = factor_of * one(*cut)
    return factor_of


def normal_values(key, dims, width, bound, pieces=(), held_as=jnp.bfloat16):
    factor_of = shard_levels(key, dims, pieces, -0.22, 0.18) if pieces else 1.0
    entries = jax.random.normal(key, dims, jnp.float32) * width * factor_of
    return jnp.minimum(jnp.maximum(entries, -bound), bound).astype(held_as)


def bell_draw_with(key, dims, spread, limit, cuts, heavy, held_as=jnp.bfloat16):
    values = spread * jax.random.normal(key, dims, jnp.float32)
    if cuts:
        values = values * shard_levels(key, dims, cuts, -0.22, 0.18)
    return jnp.clip(strengthened(values, jax.random.fold_in(key, 3), *heavy), -limit, limit).astype(held_as)


def setup_inputs(seed: int = 0) -> dict:
    key_of = jax.random.split(jax.random.key(seed), 6)
    return {
        "numerators": normal_values(key_of[0], (N_GROUP, ROWS, D), 1.0, 6.0, ((0, 8), (1, 32)), jnp.float32),
        "push_weight": jnp.clip(jnp.exp(math.log(2.0) - 1.3862944 * jax.random.uniform(key_of[1], (N_GROUP,), jnp.float32) ** shard_levels(key_of[1], (N_GROUP,), ((0, 8),), -0.2, 0.2)), 0.5, 2.0),
        "keep_share": jnp.clip(0.25 + 0.5 * jax.random.uniform(key_of[2], (N_GROUP,), jnp.float32) ** shard_levels(key_of[2], (N_GROUP,), ((0, 8),), -0.2, 0.2), 0.25, 0.75),
        "momentum": normal_values(key_of[3], (N_GROUP, ROWS, D), 0.5, 4.0, ((0, 8), (1, 32)), jnp.float32),
        "grads": bell_draw_with(key_of[4], (STEPS, N_GROUP, N_SHARD, ROWS, D), 1.0, 6.0, ((1, 8), (2, 32)), (2, 3, 32, 2.75), jnp.float32),
    }


learn_rate = 0.5
momentum_factor = 0.9


def reference(numerators, push_weight, keep_share, momentum, grads):
    values = numerators
    weight = push_weight
    buffer = momentum
    levels = int(N_GROUP).bit_length() - 1
    keep_rows = keep_share[:, None, None]
    for step in range(STEPS):
        mean = jnp.sum(grads[step].astype(jnp.float32), axis=1) / N_SHARD
        buffer = momentum_factor * buffer + mean
        values = values - learn_rate * (mean + momentum_factor * buffer)
        distance = 1 << (step % levels)
        values = keep_rows * values + jnp.roll((1.0 - keep_rows) * values, distance, axis=0)
        weight = keep_share * weight + jnp.roll((1.0 - keep_share) * weight, distance, axis=0)
    displacement = values / weight[:, None, None] - numerators / push_weight[:, None, None]
    return displacement, buffer, weight
```

```python
import jax
import jax.numpy as jnp
from jax import lax
from jax.experimental import pallas as pl
from jax.experimental.pallas import tpu as pltpu
from jax.sharding import Mesh, PartitionSpec as P

STEPS = 3
ROWS = 128
D = 5120
HALF = D // 2
X, ZL, Y, ZH, CORE = 4, 2, 4, 4, 2
GROUP = ("x", "zl")
SHARD = ("y", "zh", "core")

learn_rate = 0.5
momentum_factor = 0.9


def ring(x, axis, by):
    n = lax.axis_size(axis)
    return lax.ppermute(x, axis, [(i, (i + by) % n) for i in range(n)])


def split_kernel(where_ref, g_ref, other_ref, own_ref):
    core = where_ref[1]
    row = lax.broadcasted_iota(jnp.int32, (8, D), 0)
    for m in range(2):
        low = g_ref[0, 0, 0, 16 * m : 16 * m + 8, :]
        high = g_ref[0, 0, 0, 16 * m + 8 : 16 * m + 16, :]
        first = jnp.where(row < 4, low, pltpu.roll(high, 4, 0))
        second = jnp.where(row < 4, pltpu.roll(low, 4, 0), high)
        own_ref[0, 8 * m : 8 * m + 8, :] = jnp.where(core == 0, first, second)
        other_ref[0, 8 * m : 8 * m + 8, :] = jnp.where(core == 0, second, first)


def split_cores(where, grads, step):
    shape = jax.ShapeDtypeStruct((Y, 16, D), jnp.float32)
    out = pl.BlockSpec((1, 16, D), lambda r, w: (r, 0, 0))
    return pl.pallas_call(
        split_kernel,
        out_shape=(shape, shape),
        grid_spec=pltpu.PrefetchScalarGridSpec(
            num_scalar_prefetch=1,
            grid=(Y,),
            in_specs=[
                pl.BlockSpec((1, 1, 1, 32, D), lambda r, w: (step, 0, 0, lax.rem(w[0] + r, Y), 0))
            ],
            out_specs=(out, out),
        ),
        cost_estimate=pl.CostEstimate(flops=0, bytes_accessed=2 * ROWS * D * 4, transcendentals=0),
    )(where, grads)


def shard_mean(where, grads, step):
    zh = lax.axis_index("zh")
    other, own = split_cores(where, grads, step)
    part = own + ring(other, "core", 1)
    from_low = ring(part[2, :, :HALF], "y", 1)
    from_high = ring(part[2, :, HALF:], "y", -1)
    up = jnp.concatenate([part[1, :, :HALF] + from_low, part[1, :, HALF:]], axis=1)
    down = jnp.concatenate([part[3, :, :HALF], part[3, :, HALF:] + from_high], axis=1)
    total = part[0] + ring(up, "y", 1) + ring(down, "y", -1)
    rows = [
        lax.dynamic_slice_in_dim(total, 4 * ((zh + k) % ZH), 4, 0) for k in range(ZH)
    ]
    out = rows[0]
    for k in range(1, ZH):
        out = out + ring(rows[k], "zh", k)
    return (out / (Y * ZH * CORE))[None]


def group_weights(push_weight, keep_share):
    both = lax.all_gather(jnp.stack([push_weight, keep_share], axis=1), GROUP, axis=0, tiled=True)
    weights, keep = both[:, 0], both[:, 1]
    levels = (X * ZL).bit_length() - 1
    for step in range(STEPS):
        distance = 1 << step % levels
        weights = keep * weights + jnp.roll((1.0 - keep) * weights, distance)
    me = lax.axis_index("x") * ZL + lax.axis_index("zl")
    return lax.dynamic_slice_in_dim(weights, me, 1)


def per_device(numerators, push_weight, keep_share, momentum, grads):
    levels = (X * ZL).bit_length() - 1
    where = jnp.stack([lax.axis_index("y"), lax.axis_index("core")]).astype(jnp.int32)
    weight = group_weights(push_weight, keep_share)
    means = [shard_mean(where, grads, step) for step in range(STEPS)]
    values = numerators
    buffer = momentum
    keep_rows = keep_share[:, None, None]
    for step in range(STEPS):
        mean = means[step]
        buffer = momentum_factor * buffer + mean
        values = values - learn_rate * (mean + momentum_factor * buffer)
        sent = ring((1.0 - keep_rows) * values, GROUP, 1 << step % levels)
        values = keep_rows * values + sent
    displacement = values / weight[:, None, None] - numerators / push_weight[:, None, None]
    return (displacement, buffer, weight)


def solution(mesh):
    fine = Mesh(mesh.devices.reshape(X, ZL, Y, ZH, CORE), GROUP + SHARD)
    in_specs = (
        P(GROUP, SHARD, None),
        P(GROUP),
        P(GROUP),
        P(GROUP, SHARD, None),
        P(None, GROUP, SHARD, None, None),
    )
    out_specs = (P(GROUP, SHARD, None), P(GROUP, SHARD, None), P(GROUP))
    return jax.shard_map(
        per_device, mesh=fine, in_specs=in_specs, out_specs=out_specs, check_vma=False
    )
```

```python
import functools

import jax
import jax.numpy as jnp
from jax import lax
from jax.experimental import pallas as pl
from jax.experimental.pallas import tpu as pltpu
from jax.sharding import Mesh, PartitionSpec as P

STEPS = 3
ROWS = 128
D = 5120
HALF = D // 2
STRIP = 1024
X, ZL, Y, ZH, CORE = 4, 2, 4, 4, 2
GROUP = ("x", "zl")
SHARD = ("y", "zh", "core")

learn_rate = 0.5
momentum_factor = 0.9


def ring(x, axis, by):
    n = lax.axis_size(axis)
    return lax.ppermute(x, axis, [(i, (i + by) % n) for i in range(n)])


def split_kernel(step, g_ref, other_ref, own_ref, block, arrived):
    me, core = lax.axis_index("y"), lax.axis_index("core")
    copies = {}
    for r in (2, 1, 3, 0):
        first_row = pl.multiple_of(32 * lax.rem(me + r, Y), 32)
        copies[r] = pltpu.make_async_copy(
            g_ref.at[step, 0, 0, pl.ds(first_row, 32), :], block.at[r], arrived.at[r]
        )
        copies[r].start()
    row = lax.broadcasted_iota(jnp.int32, (8, STRIP), 0)
    for r in (2, 1, 3, 0):
        copies[r].wait()
        for m in range(2):
            for at in range(0, D, STRIP):
                columns = slice(at, at + STRIP)
                low = block[r, 16 * m : 16 * m + 8, columns]
                high = block[r, 16 * m + 8 : 16 * m + 16, columns]
                first = jnp.where(row < 4, low, pltpu.roll(high, 4, 0))
                second = jnp.where(row < 4, pltpu.roll(low, 4, 0), high)
                own_ref[r, 8 * m : 8 * m + 8, columns] = jnp.where(core == 0, first, second)
                other_ref[r, 8 * m : 8 * m + 8, columns] = jnp.where(core == 0, second, first)


def split_cores(grads, step):
    shape = pltpu.VMEM((Y, 16, D), jnp.float32)
    return pl.pallas_call(
        functools.partial(split_kernel, step),
        out_shape=(shape, shape),
        in_specs=[pl.BlockSpec(memory_space=pltpu.HBM)],
        out_specs=[pl.BlockSpec(memory_space=pltpu.VMEM)] * 2,
        scratch_shapes=[pltpu.VMEM((Y, 32, D), jnp.float32), pltpu.SemaphoreType.DMA((Y,))],
        compiler_params=pltpu.CompilerParams(vmem_limit_bytes=16 << 20),
        cost_estimate=pl.CostEstimate(flops=0, bytes_accessed=2 * ROWS * D * 4, transcendentals=0),
    )(grads)


def shard_mean(grads, step):
    zh = lax.axis_index("zh")
    other, own = split_cores(grads, step)
    part = own + ring(other, "core", 1)
    from_low = ring(part[2, :, :HALF], "y", 1)
    from_high = ring(part[2, :, HALF:], "y", -1)
    up = jnp.concatenate([part[1, :, :HALF] + from_low, part[1, :, HALF:]], axis=1)
    down = jnp.concatenate([part[3, :, :HALF], part[3, :, HALF:] + from_high], axis=1)
    total = part[0] + ring(up, "y", 1) + ring(down, "y", -1)
    rows = [
        lax.dynamic_slice_in_dim(total, 4 * ((zh + k) % ZH), 4, 0) for k in range(ZH)
    ]
    out = rows[0]
    for k in range(1, ZH):
        out = out + ring(rows[k], "zh", k)
    return (out / (Y * ZH * CORE))[None]


def per_device(numerators, push_weight, keep_share, momentum, grads):
    levels = (X * ZL).bit_length() - 1
    means = [shard_mean(grads, step) for step in range(STEPS)]
    weight = jnp.broadcast_to(push_weight[:, None, None], (1, 4, 128))
    values = jnp.concatenate([numerators, weight], axis=2)
    buffer = momentum
    keep_rows = keep_share[:, None, None]
    for step in range(STEPS):
        mean = means[step]
        buffer = momentum_factor * buffer + mean
        moved = learn_rate * (mean + momentum_factor * buffer)
        values = values - jnp.pad(moved, ((0, 0), (0, 0), (0, 128)))
        sent = ring((1.0 - keep_rows) * values, GROUP, 1 << step % levels)
        values = keep_rows * values + sent
    weight = values[:, 0, D]
    displacement = values[:, :, :D] / weight[:, None, None] - numerators / push_weight[:, None, None]
    return (displacement, buffer, weight)


def solution(mesh):
    fine = Mesh(mesh.devices.reshape(X, ZL, Y, ZH, CORE), GROUP + SHARD)
    in_specs = (
        P(GROUP, SHARD, None),
        P(GROUP),
        P(GROUP),
        P(GROUP, SHARD, None),
        P(None, GROUP, SHARD, None, None),
    )
    out_specs = (P(GROUP, SHARD, None), P(GROUP, SHARD, None), P(GROUP))
    return jax.shard_map(
        per_device, mesh=fine, in_specs=in_specs, out_specs=out_specs, check_vma=False
    )
```

```python
import functools

import jax
import jax.numpy as jnp
from jax import lax
from jax.experimental import pallas as pl
from jax.experimental.pallas import tpu as pltpu
from jax.sharding import Mesh, PartitionSpec as P

STEPS = 3
D = 5120
STRIP = 1024
X, ZL, Y, ZH, CORE = 4, 2, 4, 4, 2
GROUP = ("x", "zl")
SHARD = ("y", "zh", "core")

learn_rate = 0.5
momentum_factor = 0.9


def ring(x, axis, by):
    n = lax.axis_size(axis)
    return lax.ppermute(x, axis, [(i, (i + by) % n) for i in range(n)])


def partner(i, way):
    return i ^ 1 if way == 0 else 3 - i


def swap(x, axis, turn):
    pairs = []
    for y in range(Y):
        for zh in range(ZH):
            for core in range(CORE):
                way = core ^ turn
                to = (partner(y, way), zh) if axis == "y" else (y, partner(zh, way))
                pairs.append(((y * ZH + zh) * CORE + core, (to[0] * ZH + to[1]) * CORE + core))
    return lax.ppermute(x, SHARD, pairs)


def places(i, core):
    first, second = i ^ 1, 3 - i
    return (
        i,
        jnp.where(core == 0, second, first),
        jnp.where(core == 0, first, second),
        i ^ 2,
    )


OTHERS = (0, 2, 1, 3)


def split_kernel(step, g_ref, other_send, own_send, other_keep, own_keep, block, arrived):
    core = lax.axis_index("core")
    y_at = places(lax.axis_index("y"), core)
    z_at = places(lax.axis_index("zh"), core)
    order = (3, 2, 1, 0)
    copies = {}
    for q in order:
        first_row = pl.multiple_of(32 * y_at[q], 32)
        copies[q] = pltpu.make_async_copy(
            g_ref.at[step, 0, 0, pl.ds(first_row, 32), :], block.at[q], arrived.at[q]
        )
        copies[q].start()
    row = lax.broadcasted_iota(jnp.int32, (8, STRIP), 0)
    for q in order:
        copies[q].wait()
        own = (own_keep, own_send)[q // 2]
        other = (other_keep, other_send)[OTHERS[q] // 2]
        for at in range(0, D, STRIP):
            columns = slice(at, at + STRIP)
            top, low = [], []
            for z in range(ZH):
                rows = block[q, pl.ds(pl.multiple_of(8 * z_at[z], 8), 8), columns]
                turned = pltpu.roll(rows, 4, 0)
                top.append(jnp.where(core == 0, rows, turned))
                low.append(jnp.where(core == 0, turned, rows))
            for m in range(2):
                rows = slice(8 * m, 8 * m + 8)
                own[q % 2, rows, columns] = jnp.where(row < 4, top[2 * m], low[2 * m + 1])
                other[OTHERS[q] % 2, rows, columns] = jnp.where(row < 4, low[m], top[m + 2])


def split_cores(grads, step):
    shape = pltpu.VMEM((2, 16, D), jnp.float32)
    return pl.pallas_call(
        functools.partial(split_kernel, step),
        out_shape=(shape,) * 4,
        in_specs=[pl.BlockSpec(memory_space=pltpu.HBM)],
        out_specs=[pl.BlockSpec(memory_space=pltpu.VMEM)] * 4,
        scratch_shapes=[pltpu.VMEM((Y, 32, D), jnp.float32), pltpu.SemaphoreType.DMA((Y,))],
        compiler_params=pltpu.CompilerParams(vmem_limit_bytes=16 << 20),
        cost_estimate=pl.CostEstimate(flops=0, bytes_accessed=8 * 16 * D * 4, transcendentals=0),
    )(pltpu.with_memory_space_constraint(grads, pltpu.HBM))


def shard_mean(grads, step):
    other_send, own_send, other_keep, own_keep = split_cores(grads, step)
    send = own_send + ring(other_send, "core", 1)
    keep = own_keep + ring(other_keep, "core", 1)
    pair = keep + swap(send, "y", 0)
    total = pair[0] + swap(pair[1], "y", 1)
    pair = total[:8] + swap(total[8:], "zh", 0)
    total = pair[:4] + swap(pair[4:], "zh", 1)
    return (total / (Y * ZH * CORE))[None]


def per_device(numerators, push_weight, keep_share, momentum, grads):
    levels = (X * ZL).bit_length() - 1
    means = [shard_mean(grads, step) for step in range(STEPS)]
    weight = jnp.broadcast_to(push_weight[:, None, None], (1, 4, 128))
    values = jnp.concatenate([numerators, weight], axis=2)
    buffer = momentum
    keep_rows = keep_share[:, None, None]
    for step in range(STEPS):
        mean = means[step]
        buffer = momentum_factor * buffer + mean
        moved = learn_rate * (mean + momentum_factor * buffer)
        values = values - jnp.pad(moved, ((0, 0), (0, 0), (0, 128)))
        sent = ring((1.0 - keep_rows) * values, GROUP, 1 << step % levels)
        values = keep_rows * values + sent
    weight = values[:, 0, D]
    displacement = values[:, :, :D] / weight[:, None, None] - numerators / push_weight[:, None, None]
    return (displacement, buffer, weight)


def solution(mesh):
    fine = Mesh(mesh.devices.reshape(X, ZL, Y, ZH, CORE), GROUP + SHARD)
    in_specs = (
        P(GROUP, SHARD, None),
        P(GROUP),
        P(GROUP),
        P(GROUP, SHARD, None),
        P(None, GROUP, SHARD, None, None),
    )
    out_specs = (P(GROUP, SHARD, None), P(GROUP, SHARD, None), P(GROUP))
    return jax.shard_map(
        per_device, mesh=fine, in_specs=in_specs, out_specs=out_specs, check_vma=False
    )
```

```python
import functools

import jax
import jax.numpy as jnp
from jax import lax
from jax.experimental import pallas as pl
from jax.experimental.pallas import tpu as pltpu
from jax.sharding import Mesh, PartitionSpec as P

STEPS = 3
D = 5120
STRIP = 1024
X, ZL, Y, ZH, CORE = 4, 2, 4, 4, 2
GROUP = ("x", "zl")
SHARD = ("y", "zh", "core")

learn_rate = 0.5
momentum_factor = 0.9


def ring(x, axis, by):
    n = lax.axis_size(axis)
    return lax.ppermute(x, axis, [(i, (i + by) % n) for i in range(n)])


def partner(i, way):
    return i ^ 1 if way == 0 else 3 - i


def swap(x, axis, turn):
    pairs = []
    for y in range(Y):
        for zh in range(ZH):
            for core in range(CORE):
                way = core ^ turn
                to = (partner(y, way), zh) if axis == "y" else (y, partner(zh, way))
                pairs.append(((y * ZH + zh) * CORE + core, (to[0] * ZH + to[1]) * CORE + core))
    return lax.ppermute(x, SHARD, pairs)


def places(i, core):
    first, second = i ^ 1, 3 - i
    return (
        i,
        jnp.where(core == 0, second, first),
        jnp.where(core == 0, first, second),
        i ^ 2,
    )


OTHERS = (0, 2, 1, 3)


def split_kernel(step, g_ref, other_send, own_send, other_keep, own_keep, block, arrived):
    core = lax.axis_index("core")
    y_at = places(lax.axis_index("y"), core)
    z_at = places(lax.axis_index("zh"), core)
    order = (3, 2, 1, 0)
    copies = {}
    for q in order:
        first_row = pl.multiple_of(32 * y_at[q], 32)
        copies[q] = pltpu.make_async_copy(
            g_ref.at[step, 0, 0, pl.ds(first_row, 32), :], block.at[q], arrived.at[q]
        )
        copies[q].start()
    row = lax.broadcasted_iota(jnp.int32, (8, STRIP), 0)
    for q in order:
        copies[q].wait()
        own = (own_keep, own_send)[q // 2]
        other = (other_keep, other_send)[OTHERS[q] // 2]
        for at in range(0, D, STRIP):
            columns = slice(at, at + STRIP)
            top, low = [], []
            for z in range(ZH):
                rows = block[q, pl.ds(pl.multiple_of(8 * z_at[z], 8), 8), columns]
                turned = pltpu.roll(rows, 4, 0)
                top.append(jnp.where(core == 0, rows, turned))
                low.append(jnp.where(core == 0, turned, rows))
            for m in range(2):
                rows = slice(8 * m, 8 * m + 8)
                own[q % 2, rows, columns] = jnp.where(row < 4, top[2 * m], low[2 * m + 1])
                other[OTHERS[q] % 2, rows, columns] = jnp.where(row < 4, low[m], top[m + 2])


def split_cores(grads, step):
    shape = pltpu.VMEM((2, 16, D), jnp.float32)
    return pl.pallas_call(
        functools.partial(split_kernel, step),
        out_shape=(shape,) * 4,
        in_specs=[pl.BlockSpec(memory_space=pltpu.HBM)],
        out_specs=[pl.BlockSpec(memory_space=pltpu.VMEM)] * 4,
        scratch_shapes=[pltpu.VMEM((Y, 32, D), jnp.float32), pltpu.SemaphoreType.DMA((Y,))],
        compiler_params=pltpu.CompilerParams(vmem_limit_bytes=16 << 20),
        cost_estimate=pl.CostEstimate(flops=0, bytes_accessed=8 * 16 * D * 4, transcendentals=0),
    )(pltpu.with_memory_space_constraint(grads, pltpu.HBM))


def shard_mean(grads, step):
    other_send, own_send, other_keep, own_keep = split_cores(grads, step)
    send = own_send + ring(other_send, "core", 1)
    keep = own_keep + ring(other_keep, "core", 1)
    rows = keep + swap(send, "y", 0)
    rows = rows[:, :8] + swap(rows[:, 8:], "zh", 0)
    rows = rows[0] + swap(rows[1], "y", 1)
    rows = rows[:4] + swap(rows[4:], "zh", 1)
    return (rows / (Y * ZH * CORE))[None]


def per_device(numerators, push_weight, keep_share, momentum, grads):
    levels = (X * ZL).bit_length() - 1
    means = [shard_mean(grads, step) for step in range(STEPS)]
    weight = jnp.broadcast_to(push_weight[:, None, None], (1, 4, 128))
    values = jnp.concatenate([numerators, weight], axis=2)
    buffer = momentum
    keep_rows = keep_share[:, None, None]
    for step in range(STEPS):
        mean = means[step]
        buffer = momentum_factor * buffer + mean
        moved = learn_rate * (mean + momentum_factor * buffer)
        values = values - jnp.pad(moved, ((0, 0), (0, 0), (0, 128)))
        sent = ring((1.0 - keep_rows) * values, GROUP, 1 << step % levels)
        values = keep_rows * values + sent
    weight = values[:, 0, D]
    displacement = values[:, :, :D] / weight[:, None, None] - numerators / push_weight[:, None, None]
    return (displacement, buffer, weight)


def solution(mesh):
    fine = Mesh(mesh.devices.reshape(X, ZL, Y, ZH, CORE), GROUP + SHARD)
    in_specs = (
        P(GROUP, SHARD, None),
        P(GROUP),
        P(GROUP),
        P(GROUP, SHARD, None),
        P(None, GROUP, SHARD, None, None),
    )
    out_specs = (P(GROUP, SHARD, None), P(GROUP, SHARD, None), P(GROUP))
    return jax.shard_map(
        per_device, mesh=fine, in_specs=in_specs, out_specs=out_specs, check_vma=False
    )
```

```python
import functools

import jax
import jax.numpy as jnp
from jax import lax
from jax.experimental import pallas as pl
from jax.experimental.pallas import tpu as pltpu
from jax.sharding import Mesh, PartitionSpec as P

STEPS = 3
D = 5120
STRIP = 1024
X, ZL, Y, ZH, CORE = 4, 2, 4, 4, 2
GROUP = ("x", "zl")
SHARD = ("y", "zh", "core")

learn_rate = 0.5
momentum_factor = 0.9


def ring(x, axis, by):
    n = lax.axis_size(axis)
    return lax.ppermute(x, axis, [(i, (i + by) % n) for i in range(n)])


def partner(i, way):
    return i ^ 1 if way == 0 else 3 - i


def swap(x, axis, turn):
    pairs = []
    for y in range(Y):
        for zh in range(ZH):
            for core in range(CORE):
                way = core ^ turn
                to = (partner(y, way), zh) if axis == "y" else (y, partner(zh, way))
                pairs.append(((y * ZH + zh) * CORE + core, (to[0] * ZH + to[1]) * CORE + core))
    return lax.ppermute(x, SHARD, pairs)


def places(i, core):
    first, second = i ^ 1, 3 - i
    return (
        i,
        jnp.where(core == 0, second, first),
        jnp.where(core == 0, first, second),
        i ^ 2,
    )


OTHERS = (0, 2, 1, 3)


def split_kernel(step, g_ref, *refs):
    other_send, own_send, other_keep, own_keep, block, arrived = refs[-6:]
    core = lax.axis_index("core")
    y_at = places(lax.axis_index("y"), core)
    z_at = places(lax.axis_index("zh"), core)
    order = (3, 2, 1, 0)
    copies = {}
    for q in order:
        first_row = pl.multiple_of(32 * y_at[q], 32)
        copies[q] = pltpu.make_async_copy(
            g_ref.at[step, 0, 0, pl.ds(first_row, 32), :], block.at[q], arrived.at[q]
        )
        copies[q].start()
    row = lax.broadcasted_iota(jnp.int32, (8, STRIP), 0)
    for q in order:
        copies[q].wait()
        own = (own_keep, own_send)[q // 2]
        other = (other_keep, other_send)[OTHERS[q] // 2]
        for at in range(0, D, STRIP):
            columns = slice(at, at + STRIP)
            top, low = [], []
            for z in range(ZH):
                rows = block[q, pl.ds(pl.multiple_of(8 * z_at[z], 8), 8), columns]
                turned = pltpu.roll(rows, 4, 0)
                top.append(jnp.where(core == 0, rows, turned))
                low.append(jnp.where(core == 0, turned, rows))
            for m in range(2):
                rows = slice(8 * m, 8 * m + 8)
                own[q % 2, rows, columns] = jnp.where(row < 4, top[2 * m], low[2 * m + 1])
                other[OTHERS[q] % 2, rows, columns] = jnp.where(row < 4, low[m], top[m + 2])


def split_cores(grads, step, after):
    shape = pltpu.VMEM((2, 16, D), jnp.float32)
    return pl.pallas_call(
        functools.partial(split_kernel, step),
        out_shape=(shape,) * 4,
        in_specs=[pl.BlockSpec(memory_space=pltpu.HBM)]
        + [pl.BlockSpec(memory_space=pl.ANY)] * len(after),
        out_specs=[pl.BlockSpec(memory_space=pltpu.VMEM)] * 4,
        scratch_shapes=[pltpu.VMEM((Y, 32, D), jnp.float32), pltpu.SemaphoreType.DMA((Y,))],
        compiler_params=pltpu.CompilerParams(vmem_limit_bytes=16 << 20),
        cost_estimate=pl.CostEstimate(flops=0, bytes_accessed=8 * 16 * D * 4, transcendentals=0),
    )(pltpu.with_memory_space_constraint(grads, pltpu.HBM), *after)


def per_device(numerators, push_weight, keep_share, momentum, grads):
    keep_rows = keep_share[:, None, None]
    weight = jnp.broadcast_to(push_weight[:, None, None], (1, 4, 128))
    values = jnp.concatenate([numerators, weight], axis=2)
    start = numerators / push_weight[:, None, None]
    buffer = momentum
    other_0, own_0, otherk_0, ownk_0 = split_cores(grads, 0, ())
    come_C0 = ring(other_0, "core", 1)
    sent_0 = own_0 + come_C0
    kept_0 = ownk_0 + ring(otherk_0, "core", 1)
    other_1, own_1, otherk_1, ownk_1 = split_cores(grads, 1, ())
    come_C1 = ring(other_1, "core", 1)
    sent_1 = own_1 + come_C1
    kept_1 = ownk_1 + ring(otherk_1, "core", 1)
    other_2, own_2, otherk_2, ownk_2 = split_cores(grads, 2, ())
    come_C2 = ring(other_2, "core", 1)
    sent_2 = own_2 + come_C2
    kept_2 = ownk_2 + ring(otherk_2, "core", 1)
    ready_Y0 = sent_0
    come_Y0 = swap(ready_Y0, "y", 0)
    rows_0 = kept_0 + come_Y0
    ready_Y1 = sent_1
    come_Y1 = swap(ready_Y1, "y", 0)
    rows_1 = kept_1 + come_Y1
    ready_Y2 = sent_2
    come_Y2 = swap(ready_Y2, "y", 0)
    rows_2 = kept_2 + come_Y2
    ready_Z0 = rows_0[..., 8:, :]
    come_Z0 = swap(ready_Z0, "zh", 0)
    rows_0 = rows_0[..., :8, :] + come_Z0
    ready_Z1 = rows_1[..., 8:, :]
    come_Z1 = swap(ready_Z1, "zh", 0)
    rows_1 = rows_1[..., :8, :] + come_Z1
    ready_YY2 = rows_2[1]
    come_YY2 = swap(ready_YY2, "y", 1)
    rows_2 = rows_2[0] + come_YY2
    ready_YY0 = rows_0[1]
    come_YY0 = swap(ready_YY0, "y", 1)
    rows_0 = rows_0[0] + come_YY0
    ready_YY1 = rows_1[1]
    come_YY1 = swap(ready_YY1, "y", 1)
    rows_1 = rows_1[0] + come_YY1
    ready_Z2 = rows_2[..., 8:, :]
    come_Z2 = swap(ready_Z2, "zh", 0)
    rows_2 = rows_2[..., :8, :] + come_Z2
    ready_ZZ0 = rows_0[..., 4:, :]
    come_ZZ0 = swap(ready_ZZ0, "zh", 1)
    rows_0 = rows_0[..., :4, :] + come_ZZ0
    ready_ZZ1 = rows_1[..., 4:, :]
    come_ZZ1 = swap(ready_ZZ1, "zh", 1)
    rows_1 = rows_1[..., :4, :] + come_ZZ1
    mean = (rows_0 / (Y * ZH * CORE))[None]
    buffer = momentum_factor * buffer + mean
    moved = learn_rate * (mean + momentum_factor * buffer)
    values = values - jnp.pad(moved, ((0, 0), (0, 0), (0, 128)))
    pushed = (1.0 - keep_rows) * values
    pushed, buffer, values = lax.optimization_barrier((pushed, buffer, values))
    ready_M0 = pushed
    come_M0 = ring(pushed, GROUP, 1)
    values = keep_rows * values + come_M0
    mean = (rows_1 / (Y * ZH * CORE))[None]
    buffer = momentum_factor * buffer + mean
    moved = learn_rate * (mean + momentum_factor * buffer)
    values = values - jnp.pad(moved, ((0, 0), (0, 0), (0, 128)))
    pushed = (1.0 - keep_rows) * values
    pushed, buffer, values = lax.optimization_barrier((pushed, buffer, values))
    ready_M1 = pushed
    come_M1 = ring(pushed, GROUP, 2)
    values = keep_rows * values + come_M1
    ready_ZZ2 = rows_2[..., 4:, :]
    ready_ZZ2, *_ = lax.optimization_barrier((ready_ZZ2, ready_M0))
    come_ZZ2 = swap(ready_ZZ2, "zh", 1)
    rows_2 = rows_2[..., :4, :] + come_ZZ2
    mean = (rows_2 / (Y * ZH * CORE))[None]
    buffer = momentum_factor * buffer + mean
    moved = learn_rate * (mean + momentum_factor * buffer)
    values = values - jnp.pad(moved, ((0, 0), (0, 0), (0, 128)))
    pushed = (1.0 - keep_rows) * values
    pushed, buffer, values = lax.optimization_barrier((pushed, buffer, values))
    ready_M2 = pushed
    come_M2 = ring(pushed, GROUP, 4)
    values = keep_rows * values + come_M2
    weight = values[:, 0, D]
    displacement = values[:, :, :D] / values[:, :, D : D + 1] - start
    return (displacement, buffer, weight)


def solution(mesh):
    fine = Mesh(mesh.devices.reshape(X, ZL, Y, ZH, CORE), GROUP + SHARD)
    in_specs = (
        P(GROUP, SHARD, None),
        P(GROUP),
        P(GROUP),
        P(GROUP, SHARD, None),
        P(None, GROUP, SHARD, None, None),
    )
    out_specs = (P(GROUP, SHARD, None), P(GROUP, SHARD, None), P(GROUP))
    return jax.shard_map(
        per_device, mesh=fine, in_specs=in_specs, out_specs=out_specs, check_vma=False
    )
```

```python
import functools

import jax
import jax.numpy as jnp
from jax import lax
from jax.experimental import pallas as pl
from jax.experimental.pallas import tpu as pltpu
from jax.sharding import Mesh, PartitionSpec as P

STEPS = 3
D = 5120
STRIP = 1024
X, ZL, Y, ZH, CORE = 4, 2, 4, 4, 2
GROUP = ("x", "zl")
SHARD = ("y", "zh", "core")

learn_rate = 0.5
momentum_factor = 0.9


def ring(x, axis, by):
    n = lax.axis_size(axis)
    return lax.ppermute(x, axis, [(i, (i + by) % n) for i in range(n)])


def partner(i, way):
    return i ^ 1 if way == 0 else 3 - i


def swap(x, axis, turn):
    pairs = []
    for y in range(Y):
        for zh in range(ZH):
            for core in range(CORE):
                way = core ^ turn
                to = (partner(y, way), zh) if axis == "y" else (y, partner(zh, way))
                pairs.append(((y * ZH + zh) * CORE + core, (to[0] * ZH + to[1]) * CORE + core))
    return lax.ppermute(x, SHARD, pairs)


def places(i, core):
    first, second = i ^ 1, 3 - i
    return (
        i,
        jnp.where(core == 0, second, first),
        jnp.where(core == 0, first, second),
        i ^ 2,
    )


OTHERS = (0, 2, 1, 3)


def split_kernel(steps, g_ref, *refs):
    block, arrived = refs[-2:]
    core = lax.axis_index("core")
    y_at = places(lax.axis_index("y"), core)
    z_at = places(lax.axis_index("zh"), core)
    order = [(n, q) for n in range(len(steps)) for q in (3, 2, 1, 0)]
    copies = {}
    for n, q in order:
        first_row = pl.multiple_of(32 * y_at[q], 32)
        copies[n, q] = pltpu.make_async_copy(
            g_ref.at[steps[n], 0, 0, pl.ds(first_row, 32), :], block.at[n, q], arrived.at[n, q]
        )
        copies[n, q].start()
    row = lax.broadcasted_iota(jnp.int32, (8, STRIP), 0)
    for n, q in order:
        copies[n, q].wait()
        other_send, own_send, other_keep, own_keep = refs[4 * n : 4 * n + 4]
        own = (own_keep, own_send)[q // 2]
        other = (other_keep, other_send)[OTHERS[q] // 2]
        for at in range(0, D, STRIP):
            columns = slice(at, at + STRIP)
            top, low = [], []
            for z in range(ZH):
                rows = block[n, q, pl.ds(pl.multiple_of(8 * z_at[z], 8), 8), columns]
                turned = pltpu.roll(rows, 4, 0)
                top.append(jnp.where(core == 0, rows, turned))
                low.append(jnp.where(core == 0, turned, rows))
            for m in range(2):
                rows = slice(8 * m, 8 * m + 8)
                own[q % 2, rows, columns] = jnp.where(row < 4, top[2 * m], low[2 * m + 1])
                other[OTHERS[q] % 2, rows, columns] = jnp.where(row < 4, low[m], top[m + 2])


def split_cores(grads, steps):
    count = len(steps)
    return pl.pallas_call(
        functools.partial(split_kernel, steps),
        out_shape=(pltpu.VMEM((2, 16, D), jnp.float32),) * (4 * count),
        in_specs=[pl.BlockSpec(memory_space=pltpu.HBM)],
        out_specs=[pl.BlockSpec(memory_space=pltpu.VMEM)] * (4 * count),
        scratch_shapes=[
            pltpu.VMEM((count, Y, 32, D), jnp.float32),
            pltpu.SemaphoreType.DMA((count, Y)),
        ],
        compiler_params=pltpu.CompilerParams(vmem_limit_bytes=24 << 20),
        cost_estimate=pl.CostEstimate(
            flops=0, bytes_accessed=8 * count * 16 * D * 4, transcendentals=0
        ),
    )(pltpu.with_memory_space_constraint(grads, pltpu.HBM))


def per_device(numerators, push_weight, keep_share, momentum, grads):
    keep_rows = keep_share[:, None, None]
    weight = jnp.broadcast_to(push_weight[:, None, None], (1, 4, 128))
    values = jnp.concatenate([numerators, weight], axis=2)
    start = numerators / push_weight[:, None, None]
    buffer = momentum
    other_0, own_0, otherk_0, ownk_0 = split_cores(grads, (0,))
    come_C0 = ring(other_0, "core", 1)
    sent_0 = own_0 + come_C0
    kept_0 = ownk_0 + ring(otherk_0, "core", 1)
    later = split_cores(grads, (1, 2))
    other_1, own_1, otherk_1, ownk_1 = later[:4]
    come_C1 = ring(other_1, "core", 1)
    sent_1 = own_1 + come_C1
    kept_1 = ownk_1 + ring(otherk_1, "core", 1)
    other_2, own_2, otherk_2, ownk_2 = later[4:]
    come_C2 = ring(other_2, "core", 1)
    sent_2 = own_2 + come_C2
    kept_2 = ownk_2 + ring(otherk_2, "core", 1)
    ready_Y0 = sent_0
    come_Y0 = swap(ready_Y0, "y", 0)
    rows_0 = kept_0 + come_Y0
    ready_Y1 = sent_1
    come_Y1 = swap(ready_Y1, "y", 0)
    rows_1 = kept_1 + come_Y1
    ready_Y2 = sent_2
    ready_Y2, _ = lax.optimization_barrier((ready_Y2, ready_Y0))
    come_Y2 = swap(ready_Y2, "y", 0)
    rows_2 = kept_2 + come_Y2
    ready_Z0 = rows_0[..., 8:, :]
    come_Z0 = swap(ready_Z0, "zh", 0)
    rows_0 = rows_0[..., :8, :] + come_Z0
    ready_Z1 = rows_1[..., 8:, :]
    come_Z1 = swap(ready_Z1, "zh", 0)
    rows_1 = rows_1[..., :8, :] + come_Z1
    ready_YY2 = rows_2[1]
    come_YY2 = swap(ready_YY2, "y", 1)
    rows_2 = rows_2[0] + come_YY2
    ready_YY0 = rows_0[1]
    come_YY0 = swap(ready_YY0, "y", 1)
    rows_0 = rows_0[0] + come_YY0
    ready_YY1 = rows_1[1]
    come_YY1 = swap(ready_YY1, "y", 1)
    rows_1 = rows_1[0] + come_YY1
    ready_Z2 = rows_2[..., 8:, :]
    come_Z2 = swap(ready_Z2, "zh", 0)
    rows_2 = rows_2[..., :8, :] + come_Z2
    ready_ZZ0 = rows_0[..., 4:, :]
    come_ZZ0 = swap(ready_ZZ0, "zh", 1)
    rows_0 = rows_0[..., :4, :] + come_ZZ0
    ready_ZZ1 = rows_1[..., 4:, :]
    come_ZZ1 = swap(ready_ZZ1, "zh", 1)
    rows_1 = rows_1[..., :4, :] + come_ZZ1
    mean = (rows_0 / (Y * ZH * CORE))[None]
    buffer = momentum_factor * buffer + mean
    moved = learn_rate * (mean + momentum_factor * buffer)
    values = values - jnp.pad(moved, ((0, 0), (0, 0), (0, 128)))
    pushed = (1.0 - keep_rows) * values
    pushed, buffer, values = lax.optimization_barrier((pushed, buffer, values))
    ready_M0 = pushed
    come_M0 = ring(pushed, GROUP, 1)
    values = keep_rows * values + come_M0
    mean = (rows_1 / (Y * ZH * CORE))[None]
    buffer = momentum_factor * buffer + mean
    moved = learn_rate * (mean + momentum_factor * buffer)
    values = values - jnp.pad(moved, ((0, 0), (0, 0), (0, 128)))
    pushed = (1.0 - keep_rows) * values
    pushed, buffer, values = lax.optimization_barrier((pushed, buffer, values))
    ready_M1 = pushed
    come_M1 = ring(pushed, GROUP, 2)
    values = keep_rows * values + come_M1
    ready_ZZ2 = rows_2[..., 4:, :]
    ready_ZZ2, *_ = lax.optimization_barrier((ready_ZZ2, ready_M0))
    come_ZZ2 = swap(ready_ZZ2, "zh", 1)
    rows_2 = rows_2[..., :4, :] + come_ZZ2
    mean = (rows_2 / (Y * ZH * CORE))[None]
    buffer = momentum_factor * buffer + mean
    moved = learn_rate * (mean + momentum_factor * buffer)
    values = values - jnp.pad(moved, ((0, 0), (0, 0), (0, 128)))
    pushed = (1.0 - keep_rows) * values
    pushed, buffer, values = lax.optimization_barrier((pushed, buffer, values))
    ready_M2 = pushed
    come_M2 = ring(pushed, GROUP, 4)
    values = keep_rows * values + come_M2
    weight = values[:, 0, D]
    displacement = values[:, :, :D] / values[:, :, D : D + 1] - start
    return (displacement, buffer, weight)


def solution(mesh):
    fine = Mesh(mesh.devices.reshape(X, ZL, Y, ZH, CORE), GROUP + SHARD)
    in_specs = (
        P(GROUP, SHARD, None),
        P(GROUP),
        P(GROUP),
        P(GROUP, SHARD, None),
        P(None, GROUP, SHARD, None, None),
    )
    out_specs = (P(GROUP, SHARD, None), P(GROUP, SHARD, None), P(GROUP))
    return jax.shard_map(
        per_device, mesh=fine, in_specs=in_specs, out_specs=out_specs, check_vma=False
    )
```

```python
import functools

import jax
import jax.numpy as jnp
from jax import lax
from jax.experimental import pallas as pl
from jax.experimental.pallas import tpu as pltpu
from jax.sharding import Mesh, PartitionSpec as P

STEPS = 3
D = 5120
STRIP = 1024
X, ZL, Y, ZH, CORE = 4, 2, 4, 4, 2
GROUP = ("x", "zl")
SHARD = ("y", "zh", "core")

learn_rate = 0.5
momentum_factor = 0.9


def ring(x, axis, by):
    n = lax.axis_size(axis)
    return lax.ppermute(x, axis, [(i, (i + by) % n) for i in range(n)])


def partner(i, way):
    return i ^ 1 if way == 0 else 3 - i


def swap(x, axis, turn):
    pairs = []
    for y in range(Y):
        for zh in range(ZH):
            for core in range(CORE):
                way = core ^ turn
                to = (partner(y, way), zh) if axis == "y" else (y, partner(zh, way))
                pairs.append(((y * ZH + zh) * CORE + core, (to[0] * ZH + to[1]) * CORE + core))
    return lax.ppermute(x, SHARD, pairs)


def places(i, core):
    first, second = i ^ 1, 3 - i
    return (
        i,
        jnp.where(core == 0, second, first),
        jnp.where(core == 0, first, second),
        i ^ 2,
    )


OTHERS = (0, 2, 1, 3)


def split_kernel(steps, g_ref, *refs):
    block, arrived = refs[-2:]
    core = lax.axis_index("core")
    y_at = places(lax.axis_index("y"), core)
    z_at = places(lax.axis_index("zh"), core)
    order = [(n, q) for n in range(len(steps)) for q in (3, 2, 1, 0)]
    copies = {}
    for n, q in order:
        first_row = pl.multiple_of(32 * y_at[q], 32)
        copies[n, q] = pltpu.make_async_copy(
            g_ref.at[steps[n], 0, 0, pl.ds(first_row, 32), :], block.at[n, q], arrived.at[n, q]
        )
        copies[n, q].start()
    row = lax.broadcasted_iota(jnp.int32, (8, STRIP), 0)
    for n, q in order:
        copies[n, q].wait()
        other_send, own_send, other_keep, own_keep = refs[4 * n : 4 * n + 4]
        own = (own_keep, own_send)[q // 2]
        other = (other_keep, other_send)[OTHERS[q] // 2]
        for at in range(0, D, STRIP):
            columns = slice(at, at + STRIP)
            top, low = [], []
            for z in range(ZH):
                rows = block[n, q, pl.ds(pl.multiple_of(8 * z_at[z], 8), 8), columns]
                turned = pltpu.roll(rows, 4, 0)
                top.append(jnp.where(core == 0, rows, turned))
                low.append(jnp.where(core == 0, turned, rows))
            for m in range(2):
                rows = slice(8 * m, 8 * m + 8)
                own[q % 2, rows, columns] = jnp.where(row < 4, top[2 * m], low[2 * m + 1])
                other[OTHERS[q] % 2, rows, columns] = jnp.where(row < 4, low[m], top[m + 2])


def split_cores(grads, steps):
    count = len(steps)
    return pl.pallas_call(
        functools.partial(split_kernel, steps),
        out_shape=(pltpu.VMEM((2, 16, D), jnp.float32),) * (4 * count),
        in_specs=[pl.BlockSpec(memory_space=pltpu.HBM)],
        out_specs=[pl.BlockSpec(memory_space=pltpu.VMEM)] * (4 * count),
        scratch_shapes=[
            pltpu.VMEM((count, Y, 32, D), jnp.float32),
            pltpu.SemaphoreType.DMA((count, Y)),
        ],
        compiler_params=pltpu.CompilerParams(vmem_limit_bytes=24 << 20),
        cost_estimate=pl.CostEstimate(
            flops=0, bytes_accessed=8 * count * 16 * D * 4, transcendentals=0
        ),
    )(pltpu.with_memory_space_constraint(grads, pltpu.HBM))


def per_device(numerators, push_weight, keep_share, momentum, grads):
    keep_rows = keep_share[:, None, None]
    weight = jnp.broadcast_to(push_weight[:, None, None], (1, 4, 128))
    values = jnp.concatenate([numerators, weight], axis=2)
    start = numerators / push_weight[:, None, None]
    buffer = momentum
    other_0, own_0, otherk_0, ownk_0 = split_cores(grads, (0,))
    come_C0 = ring(other_0, "core", 1)
    sent_0 = own_0 + come_C0
    kept_0 = ownk_0 + ring(otherk_0, "core", 1)
    later = split_cores(grads, (1, 2))
    other_1, own_1, otherk_1, ownk_1 = later[:4]
    come_C1 = ring(other_1, "core", 1)
    sent_1 = own_1 + come_C1
    kept_1 = ownk_1 + ring(otherk_1, "core", 1)
    other_2, own_2, otherk_2, ownk_2 = later[4:]
    come_C2 = ring(other_2, "core", 1)
    sent_2 = own_2 + come_C2
    kept_2 = ownk_2 + ring(otherk_2, "core", 1)
    ready_Y0 = sent_0
    come_Y0 = swap(ready_Y0, "y", 0)
    rows_0 = kept_0 + come_Y0
    ready_Y1 = sent_1
    come_Y1 = swap(ready_Y1, "y", 0)
    rows_1 = kept_1 + come_Y1
    ready_Y2 = sent_2
    ready_Y2, *_ = lax.optimization_barrier((ready_Y2, ready_Y0))
    come_Y2 = swap(ready_Y2, "y", 0)
    rows_2 = kept_2 + come_Y2
    ready_Z0 = rows_0[..., 8:, :]
    come_Z0 = swap(ready_Z0, "zh", 0)
    rows_0 = rows_0[..., :8, :] + come_Z0
    ready_Z1 = rows_1[..., 8:, :]
    come_Z1 = swap(ready_Z1, "zh", 0)
    rows_1 = rows_1[..., :8, :] + come_Z1
    ready_YY2 = rows_2[1]
    come_YY2 = swap(ready_YY2, "y", 1)
    rows_2 = rows_2[0] + come_YY2
    ready_YY0 = rows_0[1]
    come_YY0 = swap(ready_YY0, "y", 1)
    rows_0 = rows_0[0] + come_YY0
    ready_YY1 = rows_1[1]
    come_YY1 = swap(ready_YY1, "y", 1)
    rows_1 = rows_1[0] + come_YY1
    ready_Z2 = rows_2[..., 8:, :]
    ready_Z2, *_ = lax.optimization_barrier((ready_Z2, ready_YY1))
    come_Z2 = swap(ready_Z2, "zh", 0)
    rows_2 = rows_2[..., :8, :] + come_Z2
    ready_ZZ0 = rows_0[..., 4:, :]
    come_ZZ0 = swap(ready_ZZ0, "zh", 1)
    rows_0 = rows_0[..., :4, :] + come_ZZ0
    ready_ZZ1 = rows_1[..., 4:, :]
    come_ZZ1 = swap(ready_ZZ1, "zh", 1)
    rows_1 = rows_1[..., :4, :] + come_ZZ1
    mean = (rows_0 / (Y * ZH * CORE))[None]
    buffer = momentum_factor * buffer + mean
    moved = learn_rate * (mean + momentum_factor * buffer)
    values = values - jnp.pad(moved, ((0, 0), (0, 0), (0, 128)))
    pushed = (1.0 - keep_rows) * values
    pushed, buffer, values = lax.optimization_barrier((pushed, buffer, values))
    ready_M0 = pushed
    come_M0 = ring(pushed, GROUP, 1)
    values = keep_rows * values + come_M0
    mean = (rows_1 / (Y * ZH * CORE))[None]
    buffer = momentum_factor * buffer + mean
    moved = learn_rate * (mean + momentum_factor * buffer)
    values = values - jnp.pad(moved, ((0, 0), (0, 0), (0, 128)))
    pushed = (1.0 - keep_rows) * values
    pushed, buffer, values = lax.optimization_barrier((pushed, buffer, values))
    ready_M1 = pushed
    come_M1 = ring(pushed, GROUP, 2)
    values = keep_rows * values + come_M1
    ready_ZZ2 = rows_2[..., 4:, :]
    ready_ZZ2, *_ = lax.optimization_barrier((ready_ZZ2, ready_M0))
    come_ZZ2 = swap(ready_ZZ2, "zh", 1)
    rows_2 = rows_2[..., :4, :] + come_ZZ2
    mean = (rows_2 / (Y * ZH * CORE))[None]
    buffer = momentum_factor * buffer + mean
    moved = learn_rate * (mean + momentum_factor * buffer)
    values = values - jnp.pad(moved, ((0, 0), (0, 0), (0, 128)))
    pushed = (1.0 - keep_rows) * values
    pushed, buffer, values = lax.optimization_barrier((pushed, buffer, values))
    ready_M2 = pushed
    come_M2 = ring(pushed, GROUP, 4)
    values = keep_rows * values + come_M2
    weight = values[:, 0, D]
    displacement = values[:, :, :D] / values[:, :, D : D + 1] - start
    return (displacement, buffer, weight)


def solution(mesh):
    fine = Mesh(mesh.devices.reshape(X, ZL, Y, ZH, CORE), GROUP + SHARD)
    in_specs = (
        P(GROUP, SHARD, None),
        P(GROUP),
        P(GROUP),
        P(GROUP, SHARD, None),
        P(None, GROUP, SHARD, None, None),
    )
    out_specs = (P(GROUP, SHARD, None), P(GROUP, SHARD, None), P(GROUP))
    return jax.shard_map(
        per_device, mesh=fine, in_specs=in_specs, out_specs=out_specs, check_vma=False
    )
```

```python
import functools

import jax
import jax.numpy as jnp
from jax import lax
from jax.experimental import pallas as pl
from jax.experimental.pallas import tpu as pltpu
from jax.sharding import Mesh, PartitionSpec as P

STEPS = 3
D = 5120
STRIP = 256
X, ZL, Y, ZH, CORE = 4, 2, 4, 4, 2
GROUP = ("x", "zl")
SHARD = ("y", "zh", "core")

learn_rate = 0.5
momentum_factor = 0.9


def ring(x, axis, by):
    n = lax.axis_size(axis)
    return lax.ppermute(x, axis, [(i, (i + by) % n) for i in range(n)])


def partner(i, way):
    return i ^ 1 if way == 0 else 3 - i


def swap(x, axis, turn):
    pairs = []
    for y in range(Y):
        for zh in range(ZH):
            for core in range(CORE):
                way = core ^ turn
                to = (partner(y, way), zh) if axis == "y" else (y, partner(zh, way))
                pairs.append(((y * ZH + zh) * CORE + core, (to[0] * ZH + to[1]) * CORE + core))
    return lax.ppermute(x, SHARD, pairs)


def places(i, core):
    first, second = i ^ 1, 3 - i
    return (
        i,
        jnp.where(core == 0, second, first),
        jnp.where(core == 0, first, second),
        i ^ 2,
    )


OTHERS = (0, 2, 1, 3)


def split_kernel(steps, g_ref, *refs):
    block, arrived = refs[-2:]
    core = lax.axis_index("core")
    y_at = places(lax.axis_index("y"), core)
    z_at = places(lax.axis_index("zh"), core)
    order = [(n, q) for n in range(len(steps)) for q in (3, 2, 1, 0)]
    copies = {}
    for n, q in order:
        first_row = pl.multiple_of(32 * y_at[q], 32)
        copies[n, q] = pltpu.make_async_copy(
            g_ref.at[steps[n], 0, 0, pl.ds(first_row, 32), :], block.at[n, q], arrived.at[n, q]
        )
        copies[n, q].start()
    row = lax.broadcasted_iota(jnp.int32, (8, STRIP), 0)
    for n, q in order:
        copies[n, q].wait()
        other_send, own_send, other_keep, own_keep = refs[4 * n : 4 * n + 4]
        own = (own_keep, own_send)[q // 2]
        other = (other_keep, other_send)[OTHERS[q] // 2]
        for at in range(0, D, STRIP):
            columns = slice(at, at + STRIP)
            top, low = [], []
            for z in range(ZH):
                rows = block[n, q, pl.ds(pl.multiple_of(8 * z_at[z], 8), 8), columns]
                turned = pltpu.roll(rows, 4, 0)
                top.append(jnp.where(core == 0, rows, turned))
                low.append(jnp.where(core == 0, turned, rows))
            for m in range(2):
                rows = slice(8 * m, 8 * m + 8)
                own[q % 2, rows, columns] = jnp.where(row < 4, top[2 * m], low[2 * m + 1])
                other[OTHERS[q] % 2, rows, columns] = jnp.where(row < 4, low[m], top[m + 2])


def split_cores(grads, steps):
    count = len(steps)
    return pl.pallas_call(
        functools.partial(split_kernel, steps),
        out_shape=(pltpu.VMEM((2, 16, D), jnp.float32),) * (4 * count),
        in_specs=[pl.BlockSpec(memory_space=pltpu.HBM)],
        out_specs=[pl.BlockSpec(memory_space=pltpu.VMEM)] * (4 * count),
        scratch_shapes=[
            pltpu.VMEM((count, Y, 32, D), jnp.float32),
            pltpu.SemaphoreType.DMA((count, Y)),
        ],
        compiler_params=pltpu.CompilerParams(vmem_limit_bytes=24 << 20),
        cost_estimate=pl.CostEstimate(
            flops=0, bytes_accessed=8 * count * 16 * D * 4, transcendentals=0
        ),
    )(pltpu.with_memory_space_constraint(grads, pltpu.HBM))


def per_device(numerators, push_weight, keep_share, momentum, grads):
    keep_rows = keep_share[:, None, None]
    weight = jnp.broadcast_to(push_weight[:, None, None], (1, 4, 128))
    values = jnp.concatenate([numerators, weight], axis=2)
    start = numerators / push_weight[:, None, None]
    buffer = momentum
    other_0, own_0, otherk_0, ownk_0 = split_cores(grads, (0,))
    come_C0 = ring(other_0, "core", 1)
    sent_0 = own_0 + come_C0
    kept_0 = ownk_0 + ring(otherk_0, "core", 1)
    later = split_cores(grads, (1, 2))
    other_1, own_1, otherk_1, ownk_1 = later[:4]
    come_C1 = ring(other_1, "core", 1)
    sent_1 = own_1 + come_C1
    kept_1 = ownk_1 + ring(otherk_1, "core", 1)
    other_2, own_2, otherk_2, ownk_2 = later[4:]
    come_C2 = ring(other_2, "core", 1)
    sent_2 = own_2 + come_C2
    kept_2 = ownk_2 + ring(otherk_2, "core", 1)
    ready_Y0 = sent_0
    come_Y0 = swap(ready_Y0, "y", 0)
    rows_0 = kept_0 + come_Y0
    ready_Y1 = sent_1
    come_Y1 = swap(ready_Y1, "y", 0)
    rows_1 = kept_1 + come_Y1
    ready_Y2 = sent_2
    ready_Y2, _ = lax.optimization_barrier((ready_Y2, ready_Y0))
    come_Y2 = swap(ready_Y2, "y", 0)
    rows_2 = kept_2 + come_Y2
    ready_Z0 = rows_0[..., 8:, :]
    come_Z0 = swap(ready_Z0, "zh", 0)
    rows_0 = rows_0[..., :8, :] + come_Z0
    ready_Z1 = rows_1[..., 8:, :]
    come_Z1 = swap(ready_Z1, "zh", 0)
    rows_1 = rows_1[..., :8, :] + come_Z1
    ready_YY2 = rows_2[1]
    come_YY2 = swap(ready_YY2, "y", 1)
    rows_2 = rows_2[0] + come_YY2
    ready_YY0 = rows_0[1]
    come_YY0 = swap(ready_YY0, "y", 1)
    rows_0 = rows_0[0] + come_YY0
    ready_YY1 = rows_1[1]
    come_YY1 = swap(ready_YY1, "y", 1)
    rows_1 = rows_1[0] + come_YY1
    ready_Z2 = rows_2[..., 8:, :]
    come_Z2 = swap(ready_Z2, "zh", 0)
    rows_2 = rows_2[..., :8, :] + come_Z2
    ready_ZZ0 = rows_0[..., 4:, :]
    come_ZZ0 = swap(ready_ZZ0, "zh", 1)
    rows_0 = rows_0[..., :4, :] + come_ZZ0
    ready_ZZ1 = rows_1[..., 4:, :]
    come_ZZ1 = swap(ready_ZZ1, "zh", 1)
    rows_1 = rows_1[..., :4, :] + come_ZZ1
    mean = (rows_0 / (Y * ZH * CORE))[None]
    buffer = momentum_factor * buffer + mean
    moved = learn_rate * (mean + momentum_factor * buffer)
    values = values - jnp.pad(moved, ((0, 0), (0, 0), (0, 128)))
    pushed = (1.0 - keep_rows) * values
    pushed, buffer, values = lax.optimization_barrier((pushed, buffer, values))
    ready_M0 = pushed
    come_M0 = ring(pushed, GROUP, 1)
    values = keep_rows * values + come_M0
    mean = (rows_1 / (Y * ZH * CORE))[None]
    buffer = momentum_factor * buffer + mean
    moved = learn_rate * (mean + momentum_factor * buffer)
    values = values - jnp.pad(moved, ((0, 0), (0, 0), (0, 128)))
    pushed = (1.0 - keep_rows) * values
    pushed, buffer, values = lax.optimization_barrier((pushed, buffer, values))
    ready_M1 = pushed
    come_M1 = ring(pushed, GROUP, 2)
    values = keep_rows * values + come_M1
    ready_ZZ2 = rows_2[..., 4:, :]
    ready_ZZ2, *_ = lax.optimization_barrier((ready_ZZ2, ready_M0))
    come_ZZ2 = swap(ready_ZZ2, "zh", 1)
    rows_2 = rows_2[..., :4, :] + come_ZZ2
    mean = (rows_2 / (Y * ZH * CORE))[None]
    buffer = momentum_factor * buffer + mean
    moved = learn_rate * (mean + momentum_factor * buffer)
    values = values - jnp.pad(moved, ((0, 0), (0, 0), (0, 128)))
    pushed = (1.0 - keep_rows) * values
    pushed, buffer, values = lax.optimization_barrier((pushed, buffer, values))
    ready_M2 = pushed
    come_M2 = ring(pushed, GROUP, 4)
    values = keep_rows * values + come_M2
    weight = values[:, 0, D]
    displacement = values[:, :, :D] / values[:, :, D : D + 1] - start
    return (displacement, buffer, weight)


def solution(mesh):
    fine = Mesh(mesh.devices.reshape(X, ZL, Y, ZH, CORE), GROUP + SHARD)
    in_specs = (
        P(GROUP, SHARD, None),
        P(GROUP),
        P(GROUP),
        P(GROUP, SHARD, None),
        P(None, GROUP, SHARD, None, None),
    )
    out_specs = (P(GROUP, SHARD, None), P(GROUP, SHARD, None), P(GROUP))
    return jax.shard_map(
        per_device, mesh=fine, in_specs=in_specs, out_specs=out_specs, check_vma=False
    )
```
